512 devices in a mesh: tm: 64 (over x_lo, z, core), feat: 8 (over x_hi, y).
Axes of the slice: x: 4 (x_hi: 2, x_lo: 2; x = x_hi * 2 + x_lo), y: 4, z: 16, core: 2. Of those that a mesh axis runs over, the one named last changes fastest.
Arguments:
- frames: bfloat16 [32768, 16384], P('tm', 'feat'), may hold values from -24 to 24, as said below
- basis: bfloat16 [16384, 256], P('feat'), may hold values from -6 to 6
Outputs:
- new_basis: float32 [16384, 256], P(('feat', 'tm'))
- reduced: float32 [256, 256], replicated
The draws below stay inside these ranges and needn't reach their ends.
Inputs may be any that keep to these rules, and one draw needn't show every extreme that they name: `frames`: frames of the trajectory.
All inputs are finite; a program needn't handle non-finite values.
Results may differ from the reference program's by a relative error of at most 0.00365.
Values may be sent and summed in bfloat16 or wider, within the bound.
No kernel may reach another device: no remote copies, remote signals or barrier semaphores. Data moves between devices by JAX's collectives and lax.ppermute only.
A program may use at most 64 MiB of HBM per device.

```python
import jax
import jax.numpy as jnp
from jax import lax

FEATS = 16384
VECS = 256
LAG = 512
TOTAL = 32768


def draw_frames(key, part):
    key = jax.random.fold_in(key, 11)
    keys = jax.random.split(key, 8)
    noise = jax.random.truncated_normal(keys[0], -3.5, 3.5, (TOTAL, FEATS), jnp.float32)
    scales = jnp.exp(jax.random.uniform(keys[1], (FEATS,), jnp.float32, jnp.log(0.04), jnp.log(0.4)))
    signs = jnp.where(jax.random.bernoulli(keys[6], 0.5, (FEATS,)), 1.0, -1.0).astype(jnp.float32)
    ratios = jax.random.uniform(keys[2], (FEATS,), jnp.float32, 45.0, 50.0)
    tilts = jax.random.uniform(keys[7], (FEATS,), jnp.float32, -2.0, 2.0)
    periods = jax.random.uniform(keys[3], (3,), jnp.float32, 2.0 * LAG, 16.0 * LAG)
    amplitudes = jax.random.uniform(keys[4], (FEATS, 3), jnp.float32, -0.7, 0.7)
    phases = jax.random.uniform(keys[5], (FEATS, 3), jnp.float32, -3.14159, 3.14159)
    times = jnp.arange(TOTAL, dtype=jnp.float32)
    slow = jnp.zeros((TOTAL, FEATS), jnp.float32)
    for mode in range(3):
        angle = 6.2831853 / periods[mode] * times[:, None] + phases[None, :, mode]
        slow = slow + amplitudes[None, :, mode] * jnp.cos(angle)
    ramp = 1.5 * times / TOTAL - 0.75
    base = signs * scales * ratios
    values = base[None, :] + scales[None, :] * (noise + slow) + (scales * tilts)[None, :] * ramp[:, None]
    return values.astype(jnp.bfloat16)


def block_levels(key, extent, shards, low, largest):
    def one(axis_at, blocks):
        heights = jax.random.uniform(jax.random.fold_in(jax.random.fold_in(key, 6), axis_at), (blocks,), jnp.float32, low / len(shards), largest / len(shards))
        return jnp.repeat(jnp.exp(heights), extent[axis_at] // blocks).reshape((-1,) + (1,) * (len(extent) - axis_at - 1))

    loudness = one(*shards[0])
    for cut in shards[1:]:
        loudness = loudness * one(*cut)
    return loudness


def bell_draw(key, shape, scale, bound, cuts=(), kind=jnp.bfloat16):
    result = jax.random.normal(key, shape, jnp.float32) * scale
    if len(cuts) > 0:
        result = block_levels(key, shape, cuts, -0.22, 0.18) * result
    return jnp.clip(result, min=-bound, max=bound).astype(kind)


def setup_inputs(seed: int = 0) -> dict:
    key_list = jax.random.split(jax.random.key(seed), 3)
    frames = draw_frames(jax.random.fold_in(key_list[2], 71), 0)
    basis = bell_draw(key_list[1], (FEATS, VECS), 1.0, 6.0, ((0, 8),))
    return dict(frames=frames, basis=basis)


def reference(frames, basis):
    total = frames.shape[0]
    vecs = basis.shape[1]
    pairs = total - LAG
    steps_t = jnp.arange(total)
    early = (steps_t < pairs).astype(jnp.bfloat16)
    late = (steps_t >= LAG).astype(jnp.bfloat16)
    count = early + late
    sums = jnp.dot(count[None, :].astype(jnp.float32), frames.astype(jnp.float32), preferred_element_type=jnp.float32)[0]
    mean = sums / (2.0 * pairs)
    basis_f = basis.astype(jnp.float32)
    offset = jnp.dot(mean, basis_f, precision=lax.Precision.HIGHEST)
    centred = (jnp.dot(frames.astype(jnp.float32), basis.astype(jnp.float32), preferred_element_type=jnp.float32) - offset[None, :]).astype(jnp.bfloat16)
    zeros_pad = jnp.zeros((LAG, vecs), jnp.bfloat16)
    following = jnp.concatenate([centred[LAG:], zeros_pad], axis=0)
    previous = jnp.concatenate([zeros_pad, centred[:total - LAG]], axis=0)
    weights = jnp.concatenate([count[:, None] * centred, early[:, None] * following, late[:, None] * previous], axis=1)
    product = lax.dot_general(frames.astype(jnp.float32), weights.astype(jnp.float32), (((0,), (0,)), ((), ())), preferred_element_type=jnp.float32)
    column_sums = jnp.sum(weights.astype(jnp.float32), axis=0)
    term = product - mean[:, None] * column_sums[None, :]
    inst = term[:, :vecs] / (2.0 * pairs)
    lagged = (term[:, vecs:2 * vecs] + term[:, 2 * vecs:]) / (2.0 * pairs)
    gram0 = jnp.dot(basis_f.T, inst, precision=lax.Precision.HIGHEST)
    gram1 = jnp.dot(basis_f.T, lagged, precision=lax.Precision.HIGHEST)
    factor = jnp.linalg.cholesky(gram0)
    new_basis = jax.scipy.linalg.solve_triangular(factor, lagged.T, lower=True).T
    half = jax.scipy.linalg.solve_triangular(factor, gram1, lower=True)
    reduced = jax.scipy.linalg.solve_triangular(factor, half.T, lower=True).T
    return (new_basis, reduced)
```

```python
import jax
import jax.numpy as jnp
from jax import lax
from jax.experimental import pallas as pl
from jax.experimental.pallas import tpu as pltpu
from jax.sharding import Mesh, PartitionSpec as P

TIME = ("xlo", "z", "core")
FEAT = ("xhi", "y")
EXACT = lax.Precision.HIGHEST


def dot(a, b, dims=((1,), (0,)), precision=EXACT):
    return lax.dot_general(
        a, b, (dims, ((), ())), precision=precision, preferred_element_type=jnp.float32
    )


def inverse_factor(block):
    nb = block.shape[0]
    lanes = lax.broadcasted_iota(jnp.int32, (8, nb), 1)
    subs = lax.broadcasted_iota(jnp.int32, (8, nb), 0)
    wide_lanes = lax.broadcasted_iota(jnp.int32, (8, 2 * nb), 1)
    wide_subs = lax.broadcasted_iota(jnp.int32, (8, 2 * nb), 0)
    tiles = [
        jnp.concatenate(
            [block[8 * g : 8 * g + 8], (lanes == subs + 8 * g).astype(jnp.float32)], axis=1
        )
        for g in range(nb // 8)
    ]
    for j in range(nb):
        g, r = divmod(j, 8)
        row = tiles[g][r : r + 1, :]
        hat = row / row[:, j : j + 1]
        for i in range(g, nb // 8):
            column = tiles[i][:, j : j + 1]
            if i == g:
                column = jnp.where(wide_subs[:, :1] > r, column, 0.0)
            tiles[i] = tiles[i] - column * hat
    out = []
    for g in range(nb // 8):
        pivots = jnp.sum(
            jnp.where(wide_lanes == wide_subs + 8 * g, tiles[g], 0.0), axis=1, keepdims=True
        )
        out.append(tiles[g] * lax.rsqrt(pivots))
    return jnp.concatenate(out, axis=0)[:, nb:]


def inverse_cholesky(a, nb):
    n = a.shape[0]
    eye = (
        lax.broadcasted_iota(jnp.int32, (n, n), 0) == lax.broadcasted_iota(jnp.int32, (n, n), 1)
    ).astype(jnp.float32)
    s = jnp.concatenate([a, eye], axis=1)
    rows = []
    for b in range(n // nb):
        t = inverse_factor(s[:nb, nb * b : nb * b + nb])
        p = dot(t, s[:nb])
        rows.append(p[:, n:])
        if nb * (b + 1) < n:
            s = s[nb:] - dot(p[:, nb * (b + 1) : n], p, ((0,), (0,)))
    return jnp.concatenate(rows, axis=0)


def whiten_kernel(blocks, frames_counted, g_ref, inv_ref, reduced_ref, edge_ref, mean_ref):
    n_feat, rows, wide = g_ref.shape
    vecs = n_feat * rows // 2
    part = vecs // n_feat
    half = n_feat // 2
    gram0 = jnp.concatenate([g_ref[k, :, :vecs] for k in range(half)], axis=0)
    gram1 = jnp.concatenate([g_ref[half + k, :, :vecs] for k in range(half)], axis=0)
    u = jnp.concatenate([g_ref[k, :blocks, vecs : vecs + part] for k in range(n_feat)], axis=1)
    z = jnp.concatenate(
        [g_ref[k, :blocks, vecs + part : vecs + 2 * part] for k in range(n_feat)], axis=1
    )
    size = frames_counted / (2.0 * blocks - 2.0)
    ids = lax.broadcasted_iota(jnp.int32, (blocks, 1), 0)
    count = jnp.where((ids == 0) | (ids == blocks - 1), 1.0, 2.0)
    share = count / (2.0 * blocks - 2.0)
    d = u - jnp.sum(share * u, axis=0, keepdims=True)
    y = z + size * d
    nothing = jnp.zeros((1, vecs), jnp.float32)

    def neighbours(x):
        return jnp.concatenate([x[1:], nothing], axis=0) + jnp.concatenate([nothing, x[:-1]], axis=0)

    edge = neighbours(y)
    edge_ref[...] = edge
    mean_ref[...] = jnp.broadcast_to(share, mean_ref.shape)
    across = ((0,), (0,))
    gram0 = (gram0 + dot(d, count * y, across) + dot(z, count * d, across)) / frames_counted
    gram1 = (gram1 + dot(z, neighbours(d), across) + dot(d, edge, across)) / frames_counted
    inv = inverse_cholesky((gram0 + gram0.T) * 0.5, 64)
    inv_ref[...] = inv
    reduced_ref[...] = dot(dot(inv, gram1), inv, ((1,), (1,)))


def finish_kernel(frames_counted, sum_ref, shift_ref, edge_ref, share_ref, inv_ref, out_ref):
    shift = shift_ref[...]
    shift = shift - jnp.sum(share_ref[:, :1] * shift, axis=0, keepdims=True)
    lagged = sum_ref[...] + dot(shift, edge_ref[...], ((0,), (0,)))
    out_ref[...] = dot(lagged / frames_counted, inv_ref[...], ((1,), (1,)))


def call(kernel, out_shape, *args):
    return pl.pallas_call(
        kernel,
        out_shape=out_shape,
        compiler_params=pltpu.CompilerParams(vmem_limit_bytes=40 << 20),
    )(*args)


def swap(x, axis):
    return lax.ppermute(x, axis, [(0, 1), (1, 0)])


def per_device(frames, basis):
    rows, width = frames.shape
    vecs = basis.shape[1]
    n_time, n_feat = lax.axis_size(TIME), lax.axis_size(FEAT)
    n_z = lax.axis_size("z")
    block, part = lax.axis_index(TIME), lax.axis_index(FEAT)
    frames_counted = 2.0 * rows * (n_time - 1)
    count = jnp.where((block == 0) | (block == n_time - 1), 1.0, 2.0)
    f32, bf16 = jnp.float32, jnp.bfloat16

    ones = jnp.ones((1, rows), bf16)
    shift = dot(ones, frames, precision=None)[0] / rows
    projected = dot(frames, basis, precision=None)
    local = jnp.mean(projected, axis=0)
    piece = rows // n_feat
    packed = jnp.concatenate(
        [
            (projected - local).reshape(n_feat, piece, vecs),
            jnp.broadcast_to(local, (n_feat, 8, vecs)),
        ],
        axis=1,
    )
    packed = jnp.sum(lax.all_to_all(packed, FEAT, 0, 0, tiled=True), axis=0)
    centred, offset = packed[:piece].astype(bf16), packed[piece]

    centred = lax.all_to_all(
        jnp.broadcast_to(centred, (n_feat, piece, vecs)), FEAT, 0, 0, tiled=True
    ).reshape(rows, vecs)
    later = lax.ppermute(centred, TIME, [(i + 1, i) for i in range(n_time - 1)])
    earlier = lax.ppermute(centred, TIME, [(i, i + 1) for i in range(n_time - 1)])

    total = jnp.sum(centred.astype(f32), axis=0)
    beside = jnp.sum(later.astype(f32), axis=0) + jnp.sum(earlier.astype(f32), axis=0)

    both = jnp.concatenate([later, earlier], axis=0)
    across = ((0,), (0,))
    lagged = dot(jnp.concatenate([frames, frames], axis=0), both, across, None)
    lagged = lagged - shift[:, None] * beside[None, :]
    owned = width // n_time
    lagged = lagged.reshape(2, n_z, 2, owned, vecs)
    core, xlo = lax.axis_index("core"), lax.axis_index("xlo")
    pick = lax.dynamic_index_in_dim
    lagged = pick(lagged, core, 2, False) + swap(pick(lagged, 1 - core, 2, False), "core")
    lagged = pick(lagged, xlo, 0, False) + swap(pick(lagged, 1 - xlo, 0, False), "xlo")
    lagged = lax.psum_scatter(
        lagged.reshape(n_z * owned, vecs), "z", scatter_dimension=0, tiled=True
    )

    gram_rows = 2 * vecs // n_feat
    first = part % (n_feat // 2) * gram_rows
    left = lax.dynamic_slice_in_dim(centred, first, gram_rows, 1)
    instant = part < n_feat // 2
    right = jnp.concatenate(
        [
            jnp.where(instant, count.astype(bf16) * centred, later),
            jnp.where(instant, jnp.zeros_like(earlier), earlier),
        ],
        axis=0,
    )
    gram = dot(jnp.concatenate([left, left], axis=0), right, across, None)
    each = gram_rows // n_time
    cols = vecs // n_feat
    sums = jnp.concatenate(
        [
            lax.dynamic_slice_in_dim(offset, part * cols, cols, 0),
            lax.dynamic_slice_in_dim(total, part * cols, cols, 0),
        ]
    )
    sent = jnp.concatenate(
        [
            gram.reshape(n_time, each * vecs),
            jnp.broadcast_to(sums, (n_time, 2 * cols)),
            shift.reshape(n_time, owned),
            jnp.zeros((n_time, -(2 * cols + owned) % 128), f32),
        ],
        axis=1,
    )
    got = lax.all_to_all(sent, TIME, 0, 0, tiled=True)
    gram = jnp.sum(got[:, : each * vecs], axis=0)
    sums = got[:, each * vecs : each * vecs + 2 * cols]
    shifts = got[:, each * vecs + 2 * cols : each * vecs + 2 * cols + owned]
    gram = lax.all_to_all(
        jnp.broadcast_to(gram, (n_time, each * vecs)), TIME, 0, 0, tiled=True
    ).reshape(gram_rows, vecs)
    sums = jnp.pad(sums, ((0, gram_rows - n_time), (0, -2 * cols % 128)))
    slices = jnp.concatenate([gram, sums], axis=1)
    slices = lax.all_to_all(
        jnp.broadcast_to(slices, (n_feat,) + slices.shape), FEAT, 0, 0, tiled=True
    )

    square = jax.ShapeDtypeStruct((vecs, vecs), f32)
    inv, reduced, edge, share = call(
        lambda *refs: whiten_kernel(n_time, frames_counted, *refs),
        [
            square,
            square,
            jax.ShapeDtypeStruct((n_time, vecs), f32),
            jax.ShapeDtypeStruct((n_time, 128), f32),
        ],
        slices,
    )
    new_basis = call(
        lambda *refs: finish_kernel(frames_counted, *refs),
        jax.ShapeDtypeStruct((owned, vecs), f32),
        lagged,
        shifts,
        edge,
        share,
        inv,
    )
    return (new_basis, reduced)


def solution(mesh):
    n_time, n_feat = mesh.devices.shape
    mesh = Mesh(mesh.devices.reshape(2, n_time // 4, 2, 2, n_feat // 2), TIME + FEAT)
    return jax.shard_map(
        per_device,
        mesh=mesh,
        in_specs=(P(TIME, FEAT), P(FEAT, None)),
        out_specs=(P(FEAT + TIME, None), P()),
        check_vma=False,
    )
```

```python
import jax
import jax.numpy as jnp
from jax import lax
from jax.experimental import pallas as pl
from jax.experimental.pallas import tpu as pltpu
from jax.sharding import Mesh, PartitionSpec as P

TIME = ("xlo", "z", "core")
FEAT = ("xhi", "y")
EXACT = lax.Precision.HIGHEST


def dot(a, b, dims=((1,), (0,)), precision=EXACT):
    return lax.dot_general(
        a, b, (dims, ((), ())), precision=precision, preferred_element_type=jnp.float32
    )


def inverse_factor(block):
    nb = block.shape[0]
    wide, count = 2 * nb, nb // 8
    lanes = lax.broadcasted_iota(jnp.int32, (8, nb), 1)
    subs = lax.broadcasted_iota(jnp.int32, (8, nb), 0)
    below = lax.broadcasted_iota(jnp.int32, (8, wide), 0)
    tiles = [
        jnp.concatenate(
            [block[8 * g : 8 * g + 8], (lanes == subs + 8 * g).astype(jnp.float32)], axis=1
        )
        for g in range(count)
    ]
    out = []
    for g in range(count):
        spread = [
            [jnp.broadcast_to(tiles[i][:, 8 * g + k : 8 * g + k + 1], (8, wide)) for i in range(g, count)]
            for k in range(8)
        ]
        rows = tiles[g]
        for r in range(0, 8, 2):
            c0, c1 = spread[r], spread[r + 1]
            p, q, s = c0[0][r : r + 1], c1[0][r : r + 1], c1[0][r + 1 : r + 2]
            det = p * s - q * q
            inv = 1.0 / det
            pi, qi, si = p * inv, q * inv, s * inv
            for k in range(r + 2, 8):
                x, y = spread[k][0][r : r + 1], spread[k][0][r + 1 : r + 2]
                gx, gy = si * x - qi * y, pi * y - qi * x
                for i in range(count - g):
                    spread[k][i] = spread[k][i] - (c0[i] * gx + c1[i] * gy)
            a, b = rows[r : r + 1], rows[r + 1 : r + 2]
            v = p * b - q * a
            ga, gb = si * a - qi * b, v * inv
            out.append(a * lax.rsqrt(p))
            out.append(v * lax.rsqrt(p * det))
            if r < 6:
                keep = below > r + 1
                rows = rows - (jnp.where(keep, c0[0], 0.0) * ga + jnp.where(keep, c1[0], 0.0) * gb)
            for i in range(g + 1, count):
                tiles[i] = tiles[i] - (c0[i - g] * ga + c1[i - g] * gb)
    return jnp.concatenate(out, axis=0)[:, nb:]


def inverse_cholesky(a, nb):
    n = a.shape[0]
    eye = lax.broadcasted_iota(jnp.int32, (n, n), 0) == lax.broadcasted_iota(jnp.int32, (n, n), 1)
    diagonal = jnp.where(eye, a, 0.0)
    down = lax.rsqrt(jnp.sum(diagonal, axis=1, keepdims=True))
    along = lax.rsqrt(jnp.sum(diagonal, axis=0, keepdims=True))
    s = jnp.concatenate([a * down * along, eye.astype(jnp.float32)], axis=1)
    rows = []
    for b in range(n // nb):
        t = inverse_factor(s[:nb, nb * b : nb * b + nb])
        p = dot(t, s[:nb])
        rows.append(p[:, n:])
        if nb * (b + 1) < n:
            s = s[nb:] - dot(p[:, nb * (b + 1) : n], p, ((0,), (0,)))
    return jnp.concatenate(rows, axis=0) * along


def whiten_kernel(blocks, frames_counted, g_ref, inv_ref, reduced_ref, edge_ref, mean_ref):
    n_feat, rows, wide = g_ref.shape
    vecs = n_feat * rows // 2
    part = vecs // n_feat
    half = n_feat // 2
    gram0 = jnp.concatenate([g_ref[k, :, :vecs] for k in range(half)], axis=0)
    gram1 = jnp.concatenate([g_ref[half + k, :, :vecs] for k in range(half)], axis=0)
    u = jnp.concatenate([g_ref[k, :blocks, vecs : vecs + part] for k in range(n_feat)], axis=1)
    z = jnp.concatenate(
        [g_ref[k, :blocks, vecs + part : vecs + 2 * part] for k in range(n_feat)], axis=1
    )
    size = frames_counted / (2.0 * blocks - 2.0)
    ids = lax.broadcasted_iota(jnp.int32, (blocks, 1), 0)
    count = jnp.where((ids == 0) | (ids == blocks - 1), 1.0, 2.0)
    share = count / (2.0 * blocks - 2.0)
    d = u - jnp.sum(share * u, axis=0, keepdims=True)
    y = z + size * d
    nothing = jnp.zeros((1, vecs), jnp.float32)

    def neighbours(x):
        return jnp.concatenate([x[1:], nothing], axis=0) + jnp.concatenate([nothing, x[:-1]], axis=0)

    edge = neighbours(y)
    edge_ref[...] = edge
    mean_ref[...] = jnp.broadcast_to(share, mean_ref.shape)
    across = ((0,), (0,))
    gram0 = (gram0 + dot(d, count * y, across) + dot(z, count * d, across)) / frames_counted
    gram1 = (gram1 + dot(z, neighbours(d), across) + dot(d, edge, across)) / frames_counted
    inv = inverse_cholesky((gram0 + gram0.T) * 0.5, 64)
    inv_ref[...] = inv
    reduced_ref[...] = dot(dot(inv, gram1), inv, ((1,), (1,)))


def finish_kernel(frames_counted, sum_ref, shift_ref, edge_ref, share_ref, inv_ref, out_ref):
    shift = shift_ref[...]
    shift = shift - jnp.sum(share_ref[:, :1] * shift, axis=0, keepdims=True)
    lagged = jnp.sum(sum_ref[...].astype(jnp.float32), axis=0) + dot(shift, edge_ref[...], ((0,), (0,)))
    out_ref[...] = dot(lagged / frames_counted, inv_ref[...], ((1,), (1,)))


def project_kernel(frames_ref, basis_ref, packed_ref):
    step, steps = pl.program_id(0), pl.num_programs(0)
    pieces, tall, vecs = packed_ref.shape
    piece = tall - 8
    each = pieces // steps
    block = dot(frames_ref[...], basis_ref[...], precision=None)
    packed_ref[pl.ds(step * each, each), :piece] = block.reshape(each, piece, vecs)

    @pl.when(step == steps - 1)
    def _():
        values = packed_ref[:, :piece]
        local = jnp.sum(jnp.sum(values, axis=0), axis=0, keepdims=True) / (pieces * piece)
        packed_ref[:, :piece] = values - local[None]
        packed_ref[:, piece:] = jnp.broadcast_to(local[None], (pieces, 8, vecs))


def shift_kernel(frames_ref, out_ref):
    n_time, lanes = out_ref.shape
    rows, width = frames_ref.shape
    owned = width // n_time
    step = width // 4
    hit = lax.broadcasted_iota(jnp.int32, (owned, lanes), 0) == lax.broadcasted_iota(
        jnp.int32, (owned, lanes), 1
    )
    ones = jnp.ones((rows, lanes), jnp.bfloat16)
    for i in range(4):
        sums = dot(frames_ref[:, i * step : (i + 1) * step], ones, ((0,), (0,)), None)
        sums = jnp.where(hit[None], sums.reshape(step // owned, owned, lanes), 0.0)
        rows_here = n_time // 4
        out_ref[i * rows_here : (i + 1) * rows_here] = jnp.sum(sums, axis=1) / rows


def collect_kernel(got_ref, centred_ref, offset_ref):
    piece = centred_ref.shape[1]
    total = jnp.sum(got_ref[...], axis=0)
    offset_ref[...] = total[piece:]
    centred_ref[...] = jnp.broadcast_to(total[:piece].astype(jnp.bfloat16)[None], centred_ref.shape)


def gram_kernel(
    place_ref, centred_ref, first_ref, second_ref, offset_ref, shift_ref, sent_ref, beside_ref, gram_ref
):
    n_time, each, wide = sent_ref.shape
    vecs = gram_ref.shape[0]
    part, n_feat, count = place_ref[0], place_ref[1], place_ref[2]
    half = n_feat // 2
    across = ((0,), (0,))
    first, second = first_ref[...], second_ref[...]
    beside = jnp.sum(first.astype(jnp.float32), axis=0, keepdims=True) + jnp.sum(
        second.astype(jnp.float32), axis=0, keepdims=True
    )
    beside_ref[...] = jnp.broadcast_to(beside, beside_ref.shape)

    @pl.when(part < half)
    def _():
        gram_ref[...] = count.astype(jnp.float32) * dot(
            centred_ref[...], centred_ref[...], across, None
        )

    @pl.when(part >= half)
    def _():
        gram_ref[...] = dot(centred_ref[...], first, across, None) + dot(
            centred_ref[...], second, across, None
        )

    rows = n_time * each
    mine = gram_ref[pl.ds(pl.multiple_of(lax.rem(part, half) * rows, rows), rows), :]
    part_cols = rows // 2
    total = jnp.sum(centred_ref[...].astype(jnp.float32), axis=0, keepdims=True)
    both = jnp.concatenate(
        [offset_ref[:4], jnp.broadcast_to(total, (4, vecs))], axis=0
    )
    both = pltpu.roll(both, lax.rem(n_feat - part, n_feat) * part_cols, 1)[:, :part_cols]
    extra = jnp.concatenate(
        [
            jnp.broadcast_to(both[:1], (n_time, part_cols)),
            jnp.broadcast_to(both[4:5], (n_time, part_cols)),
            shift_ref[:, : wide - vecs - 2 * part_cols],
        ],
        axis=1,
    )
    for i in range(n_time):
        sent_ref[i, :, :vecs] = mine[i * each : (i + 1) * each]
        sent_ref[i, :, vecs:] = jnp.broadcast_to(extra[i : i + 1], (each, wide - vecs))


def total_kernel(got_ref, row_ref, sums_ref, shift_ref):
    n_time, each, vecs = row_ref.shape
    total = got_ref[0, :, :vecs]
    for i in range(1, n_time):
        total = total + got_ref[i, :, :vecs]
    low = vecs + sums_ref.shape[1]
    for i in range(n_time):
        row_ref[i] = total
        sums_ref[i : i + 1] = got_ref[i, :1, vecs:low]
        shift_ref[i : i + 1] = got_ref[i, :1, low : low + shift_ref.shape[1]]


def slices_kernel(rows_ref, sums_ref, out_ref):
    n_feat, height, wide = out_ref.shape
    n_time, each, vecs = rows_ref.shape
    for i in range(n_time):
        out_ref[0, i * each : (i + 1) * each, :vecs] = rows_ref[i]
    side = jnp.zeros((n_time, wide - vecs - sums_ref.shape[1]), jnp.float32)
    out_ref[0, :n_time, vecs:] = jnp.concatenate([sums_ref[...], side], axis=1)
    if height > n_time:
        out_ref[0, n_time:, vecs:] = jnp.zeros((height - n_time, wide - vecs), jnp.float32)
    for k in range(1, n_feat):
        out_ref[k] = out_ref[0]


def contract_kernel(core_ref, frames_ref, first_ref, second_ref, beside_ref, kept_ref, given_ref, all_ref):
    owned = kept_ref.shape[1]
    rows, width = frames_ref.shape
    step = 8 * owned
    across = ((0,), (0,))
    beside = beside_ref[:1] / rows
    ones = jnp.ones((rows, 128), jnp.bfloat16)
    for i in range(width // step):
        frames = frames_ref[:, i * step : (i + 1) * step]
        sums = dot(frames, first_ref[...], across, None) + dot(frames, second_ref[...], across, None)
        total = dot(frames, ones, across, None)
        total = jnp.concatenate([total] * (sums.shape[1] // 128), axis=1)
        sums = sums - total * beside
        all_ref[4 * i : 4 * i + 4] = sums.reshape(4, 2, owned, sums.shape[1])
    core = core_ref[0]
    kept_ref[...] = all_ref[:, core]
    given_ref[...] = all_ref[:, 1 - core]


def halve_kernel(xlo_ref, kept_ref, got_ref, mine_ref, given_ref):
    xlo = xlo_ref[0]
    half = mine_ref.shape[0]
    own, other = pl.ds(xlo * half, half), pl.ds((1 - xlo) * half, half)
    mine_ref[...] = kept_ref[own] + got_ref[own]
    given_ref[...] = kept_ref[other] + got_ref[other]


def call(kernel, out_shape, *args, scalars=0, scratch=(), flops=0):
    vmem = pl.BlockSpec(memory_space=pltpu.VMEM)
    scalar = pl.BlockSpec(memory_space=pltpu.SMEM)
    return pl.pallas_call(
        kernel,
        out_shape=out_shape,
        in_specs=[scalar if i < scalars else vmem for i in range(len(args))],
        out_specs=jax.tree.map(lambda _: vmem, out_shape),
        scratch_shapes=list(scratch),
        cost_estimate=pl.CostEstimate(flops=flops, bytes_accessed=0, transcendentals=0),
        compiler_params=pltpu.CompilerParams(vmem_limit_bytes=40 << 20),
    )(*args)


def swap(x, axis):
    return lax.ppermute(x, axis, [(0, 1), (1, 0)])


def per_device(frames, basis):
    rows, width = frames.shape
    vecs = basis.shape[1]
    n_time, n_feat = lax.axis_size(TIME), lax.axis_size(FEAT)
    n_z = lax.axis_size("z")
    block, part = lax.axis_index(TIME), lax.axis_index(FEAT)
    frames_counted = 2.0 * rows * (n_time - 1)
    count = jnp.where((block == 0) | (block == n_time - 1), 1.0, 2.0)
    f32, bf16 = jnp.float32, jnp.bfloat16

    piece = rows // n_feat
    owned = width // n_time
    steps = 4
    packed = pl.pallas_call(
        project_kernel,
        grid=(steps,),
        in_specs=[
            pl.BlockSpec((rows // steps, width), lambda i: (i, 0)),
            pl.BlockSpec((width, vecs), lambda i: (0, 0)),
        ],
        out_specs=pl.BlockSpec((n_feat, piece + 8, vecs), lambda i: (0, 0, 0)),
        out_shape=jax.ShapeDtypeStruct((n_feat, piece + 8, vecs), f32),
        compiler_params=pltpu.CompilerParams(vmem_limit_bytes=56 << 20),
    )(frames, basis)
    shift = call(shift_kernel, jax.ShapeDtypeStruct((n_time, 128), f32), frames)
    packed = lax.all_to_all(packed, FEAT, 0, 0, tiled=True)

    centred, offset = call(
        collect_kernel,
        [
            jax.ShapeDtypeStruct((n_feat, piece, vecs), bf16),
            jax.ShapeDtypeStruct((8, vecs), f32),
        ],
        packed,
    )
    centred = lax.all_to_all(centred, FEAT, 0, 0, tiled=True).reshape(rows, vecs)
    pairs = [(i, i + 1) for i in range(1, n_time - 1, 2)]
    across_chips = lax.ppermute(centred, TIME, pairs + [(b, a) for a, b in pairs])
    on_chip = swap(centred, "core")

    gram_rows = 2 * vecs // n_feat
    each = gram_rows // n_time
    cols = vecs // n_feat
    wide = vecs - (-(2 * cols + owned) // 128) * 128
    sent, beside = call(
        gram_kernel,
        [
            jax.ShapeDtypeStruct((n_time, each, wide), f32),
            jax.ShapeDtypeStruct((8, vecs), f32),
        ],
        jnp.stack([part, jnp.int32(n_feat), count.astype(jnp.int32)]),
        centred,
        on_chip,
        across_chips,
        offset,
        shift,
        scalars=1,
        scratch=[pltpu.VMEM((vecs, vecs), f32)],
    )
    got = lax.all_to_all(sent, TIME, 0, 0, tiled=True)
    gram, sums, shifts = call(
        total_kernel,
        [
            jax.ShapeDtypeStruct((n_time, each, vecs), f32),
            jax.ShapeDtypeStruct((n_time, 2 * cols), f32),
            jax.ShapeDtypeStruct((n_time, owned), f32),
        ],
        got,
    )
    gram = lax.all_to_all(gram, TIME, 0, 0, tiled=True)
    slices = call(
        slices_kernel,
        jax.ShapeDtypeStruct((n_feat, gram_rows, wide), f32),
        gram,
        sums,
    )
    slices = lax.all_to_all(slices, FEAT, 0, 0, tiled=True)

    half = jax.ShapeDtypeStruct((2 * n_z, owned, vecs), f32)
    kept, given = call(
        contract_kernel,
        [half, half],
        lax.axis_index("core")[None],
        frames,
        on_chip,
        across_chips,
        beside,
        scalars=1,
        scratch=[pltpu.VMEM((2 * n_z, 2, owned, vecs), f32)],
        flops=4 * rows * width * vecs,
    )
    half = jax.ShapeDtypeStruct((n_z, owned, vecs), f32)
    mine, given = call(
        halve_kernel,
        [half, half],
        lax.axis_index("xlo")[None],
        kept,
        swap(given, "core"),
        scalars=1,
    )
    lagged = (mine + swap(given, "xlo")).astype(bf16)
    lagged = lax.all_to_all(lagged, "z", 0, 0, tiled=True)

    square = jax.ShapeDtypeStruct((vecs, vecs), f32)
    inv, reduced, edge, share = call(
        lambda *refs: whiten_kernel(n_time, frames_counted, *refs),
        [
            square,
            square,
            jax.ShapeDtypeStruct((n_time, vecs), f32),
            jax.ShapeDtypeStruct((n_time, 128), f32),
        ],
        slices,
        flops=11 * 10**9,
    )
    new_basis = call(
        lambda *refs: finish_kernel(frames_counted, *refs),
        jax.ShapeDtypeStruct((owned, vecs), f32),
        lagged,
        shifts,
        edge,
        share,
        inv,
        flops=10**9,
    )
    return (new_basis, reduced)


def solution(mesh):
    n_time, n_feat = mesh.devices.shape
    mesh = Mesh(mesh.devices.reshape(2, n_time // 4, 2, 2, n_feat // 2), TIME + FEAT)
    return jax.shard_map(
        per_device,
        mesh=mesh,
        in_specs=(P(TIME, FEAT), P(FEAT, None)),
        out_specs=(P(FEAT + TIME, None), P()),
        check_vma=False,
    )
```

```python
import jax
import jax.numpy as jnp
from jax import lax
from jax.experimental import pallas as pl
from jax.experimental.pallas import tpu as pltpu
from jax.sharding import Mesh, PartitionSpec as P

TIME = ("xlo", "zh", "zl", "core")
FEAT = ("xhi", "y")
EXACT = lax.Precision.HIGHEST


def dot(a, b, dims=((1,), (0,)), precision=EXACT):
    return lax.dot_general(
        a, b, (dims, ((), ())), precision=precision, preferred_element_type=jnp.float32
    )


def inverse_factor(block):
    nb = block.shape[0]
    wide, count = 2 * nb, nb // 8
    lanes = lax.broadcasted_iota(jnp.int32, (8, nb), 1)
    subs = lax.broadcasted_iota(jnp.int32, (8, nb), 0)
    below = lax.broadcasted_iota(jnp.int32, (8, wide), 0)
    tiles = [
        jnp.concatenate(
            [block[8 * g : 8 * g + 8], (lanes == subs + 8 * g).astype(jnp.float32)], axis=1
        )
        for g in range(count)
    ]
    out = []
    for g in range(count):
        spread = [
            [jnp.broadcast_to(tiles[i][:, 8 * g + k : 8 * g + k + 1], (8, wide)) for i in range(g, count)]
            for k in range(8)
        ]
        rows = tiles[g]
        for r in range(0, 8, 2):
            c0, c1 = spread[r], spread[r + 1]
            p, q, s = c0[0][r : r + 1], c1[0][r : r + 1], c1[0][r + 1 : r + 2]
            det = p * s - q * q
            inv = 1.0 / det
            pi, qi, si = p * inv, q * inv, s * inv
            for k in range(r + 2, 8):
                x, y = spread[k][0][r : r + 1], spread[k][0][r + 1 : r + 2]
                gx, gy = si * x - qi * y, pi * y - qi * x
                for i in range(count - g):
                    spread[k][i] = spread[k][i] - (c0[i] * gx + c1[i] * gy)
            a, b = rows[r : r + 1], rows[r + 1 : r + 2]
            v = p * b - q * a
            ga, gb = si * a - qi * b, v * inv
            out.append(a * lax.rsqrt(p))
            out.append(v * lax.rsqrt(p * det))
            if r < 6:
                keep = below > r + 1
                rows = rows - (jnp.where(keep, c0[0], 0.0) * ga + jnp.where(keep, c1[0], 0.0) * gb)
            for i in range(g + 1, count):
                tiles[i] = tiles[i] - (c0[i - g] * ga + c1[i - g] * gb)
    return jnp.concatenate(out, axis=0)[:, nb:]


def inverse_cholesky(a, nb):
    n = a.shape[0]
    eye = lax.broadcasted_iota(jnp.int32, (n, n), 0) == lax.broadcasted_iota(jnp.int32, (n, n), 1)
    diagonal = jnp.where(eye, a, 0.0)
    down = lax.rsqrt(jnp.sum(diagonal, axis=1, keepdims=True))
    along = lax.rsqrt(jnp.sum(diagonal, axis=0, keepdims=True))
    s = jnp.concatenate([a * down * along, eye.astype(jnp.float32)], axis=1)
    rows = []
    for b in range(n // nb):
        t = inverse_factor(s[:nb, nb * b : nb * b + nb])
        p = dot(t, s[:nb])
        rows.append(p[:, n:])
        if nb * (b + 1) < n:
            s = s[nb:] - dot(p[:, nb * (b + 1) : n], p, ((0,), (0,)))
    return jnp.concatenate(rows, axis=0) * along


def whiten_kernel(blocks, frames_counted, g_ref, inv_ref, reduced_ref, edge_ref, mean_ref):
    peers, height, vecs = g_ref.shape
    n_feat, rows = peers // 2, height - 8
    part, half = vecs // n_feat, n_feat // 2

    def joined(start):
        return jnp.concatenate(
            [g_ref[x * n_feat + start + k, :rows] for k in range(half) for x in range(2)], axis=0
        )

    def sums(start):
        columns = []
        for k in range(n_feat):
            side = [g_ref[x * n_feat + k, rows:] for x in range(2)]
            columns.append(
                jnp.concatenate(
                    [
                        side[x][:, 2 * part * g + start : 2 * part * g + start + part]
                        for x in range(2)
                        for g in range(blocks // 16)
                    ],
                    axis=0,
                )
            )
        return jnp.concatenate(columns, axis=1)

    gram0, gram1 = joined(0), joined(half)
    u, z = sums(0), sums(part)
    size = frames_counted / (2.0 * blocks - 2.0)
    ids = lax.broadcasted_iota(jnp.int32, (blocks, 1), 0)
    count = jnp.where((ids == 0) | (ids == blocks - 1), 1.0, 2.0)
    share = count / (2.0 * blocks - 2.0)
    d = u - jnp.sum(share * u, axis=0, keepdims=True)
    y = z + size * d
    nothing = jnp.zeros((1, vecs), jnp.float32)

    def neighbours(x):
        return jnp.concatenate([x[1:], nothing], axis=0) + jnp.concatenate([nothing, x[:-1]], axis=0)

    edge = neighbours(y)
    edge_ref[...] = edge
    mean_ref[...] = jnp.broadcast_to(share, mean_ref.shape)
    across = ((0,), (0,))
    gram0 = (gram0 + dot(d, count * y, across) + dot(z, count * d, across)) / frames_counted
    gram1 = (gram1 + dot(z, neighbours(d), across) + dot(d, edge, across)) / frames_counted
    inv = inverse_cholesky((gram0 + gram0.T) * 0.5, 64)
    inv_ref[...] = inv
    reduced_ref[...] = dot(dot(inv, gram1), inv, ((1,), (1,)))


def finish_kernel(frames_counted, sum_ref, shift_ref, edge_ref, share_ref, inv_ref, out_ref):
    shift = shift_ref[...]
    shift = shift - jnp.sum(share_ref[:, :1] * shift, axis=0, keepdims=True)
    lagged = jnp.sum(sum_ref[...].astype(jnp.float32), axis=0) + dot(shift, edge_ref[...], ((0,), (0,)))
    out_ref[...] = dot(lagged / frames_counted, inv_ref[...], ((1,), (1,)))


def shift_kernel(frames_ref, out_ref):
    n_time, lanes = out_ref.shape
    rows, width = frames_ref.shape
    owned = width // n_time
    step = width // 4
    hit = lax.broadcasted_iota(jnp.int32, (owned, lanes), 0) == lax.broadcasted_iota(
        jnp.int32, (owned, lanes), 1
    )
    ones = jnp.ones((rows, lanes), jnp.bfloat16)
    for i in range(4):
        sums = dot(frames_ref[:, i * step : (i + 1) * step], ones, ((0,), (0,)), None)
        sums = jnp.where(hit[None], sums.reshape(step // owned, owned, lanes), 0.0)
        rows_here = n_time // 4
        out_ref[i * rows_here : (i + 1) * rows_here] = jnp.sum(sums, axis=1) / rows


def collect_kernel(got_ref, centred_ref, offset_ref):
    piece = centred_ref.shape[1]
    total = jnp.sum(got_ref[...].astype(jnp.float32), axis=0)
    offset = jnp.sum(total[piece:], axis=0, keepdims=True)
    offset_ref[...] = jnp.broadcast_to(offset, offset_ref.shape)
    centred_ref[...] = jnp.broadcast_to(total[:piece].astype(jnp.bfloat16)[None], centred_ref.shape)


def gram_kernel(
    place_ref, centred_ref, first_ref, second_ref, offset_ref, shift_ref, sent_ref, beside_ref, gram_ref
):
    n_time, each, wide = sent_ref.shape
    vecs = gram_ref.shape[0]
    part, n_feat, count = place_ref[0], place_ref[1], place_ref[2]
    half = n_feat // 2
    across = ((0,), (0,))
    first, second = first_ref[1 - place_ref[3]], second_ref[...]
    beside = jnp.sum(first.astype(jnp.float32), axis=0, keepdims=True) + jnp.sum(
        second.astype(jnp.float32), axis=0, keepdims=True
    )
    beside_ref[...] = jnp.broadcast_to(beside, beside_ref.shape)

    @pl.when(part < half)
    def _():
        gram_ref[...] = count.astype(jnp.float32) * dot(
            centred_ref[...], centred_ref[...], across, None
        )

    @pl.when(part >= half)
    def _():
        gram_ref[...] = dot(centred_ref[...], first, across, None) + dot(
            centred_ref[...], second, across, None
        )

    rows = n_time * each
    mine = gram_ref[pl.ds(pl.multiple_of(lax.rem(part, half) * rows, rows), rows), :]
    part_cols = rows // 2
    total = jnp.sum(centred_ref[...].astype(jnp.float32), axis=0, keepdims=True)
    both = jnp.concatenate(
        [offset_ref[:4], jnp.broadcast_to(total, (4, vecs))], axis=0
    )
    both = pltpu.roll(both, lax.rem(n_feat - part, n_feat) * part_cols, 1)[:, :part_cols]
    extra = jnp.concatenate(
        [
            jnp.broadcast_to(both[:1], (n_time, part_cols)),
            jnp.broadcast_to(both[4:5], (n_time, part_cols)),
            shift_ref[:, : wide - vecs - 2 * part_cols],
        ],
        axis=1,
    )
    for i in range(n_time):
        sent_ref[i, :, :vecs] = mine[i * each : (i + 1) * each]
        sent_ref[i, :, vecs:] = jnp.broadcast_to(extra[i : i + 1], (each, wide - vecs))


def total_kernel(got_ref, row_ref, sums_ref, shift_ref):
    copies, _, vecs = row_ref.shape
    n_time = sums_ref.shape[0]
    total = got_ref[0, :, :vecs]
    for i in range(1, n_time):
        total = total + got_ref[i, :, :vecs]
    for i in range(copies):
        row_ref[i] = total
    low = vecs + sums_ref.shape[1]
    for i in range(n_time):
        sums_ref[i : i + 1] = got_ref[i, :1, vecs:low]
        shift_ref[i : i + 1] = got_ref[i, :1, low : low + shift_ref.shape[1]]


def slices_kernel(xlo_ref, rows_ref, sums_ref, _, out_ref):
    copies, height, vecs = out_ref.shape
    blocks, each, _ = rows_ref.shape
    for i in range(blocks):
        out_ref[0, i * each : (i + 1) * each] = rows_ref[i]
    first = pl.multiple_of(xlo_ref[0] * blocks, 8)
    side = [sums_ref[pl.ds(first + 8 * g, 8), :] for g in range(blocks // 8)]
    rest = vecs - len(side) * sums_ref.shape[1]
    side = side + [jnp.zeros((8, rest), jnp.float32)] if rest else side
    out_ref[0, height - 8 :] = jnp.concatenate(side, axis=1)
    for k in range(1, copies):
        out_ref[k] = out_ref[0]


def contract_kernel(core_ref, frames_ref, first_ref, second_ref, beside_ref, kept_ref, given_ref):
    owned, vecs = kept_ref.shape[1:]
    rows, width = frames_ref.shape
    groups = 4
    core = core_ref[0]
    beside = beside_ref[:1] / rows
    right = jnp.concatenate(
        [first_ref[1 - core], second_ref[...], jnp.ones((rows, 128), jnp.bfloat16)], axis=1
    )
    step = 2 * groups * owned
    for i in range(width // step):
        sums = dot(frames_ref[:, i * step : (i + 1) * step], right, ((0,), (0,)), None)
        total = jnp.concatenate([sums[:, 2 * vecs :]] * (vecs // 128), axis=1)
        sums = sums[:, :vecs] + sums[:, vecs : 2 * vecs] - total * beside
        sums = sums.reshape(groups, 2, owned, vecs)
        low, high = sums[:, 0], sums[:, 1]
        part = slice(i * groups, (i + 1) * groups)
        kept_ref[part] = jnp.where(core == 0, low, high)
        given_ref[part] = jnp.where(core == 0, high, low).astype(given_ref.dtype)


def halve_kernel(axis, place_ref, kept_ref, got_ref, mine_ref, given_ref):
    def at(which):
        return (slice(None),) * axis + (which,)

    own, other = at(place_ref[0]), at(1 - place_ref[0])
    mine_ref[...] = kept_ref[own] + got_ref[own].astype(jnp.float32)
    given_ref[...] = (kept_ref[other] + got_ref[other].astype(jnp.float32)).astype(given_ref.dtype)


def call(kernel, out_shape, *args, scalars=0, unread=0, scratch=(), flops=0):
    vmem = pl.BlockSpec(memory_space=pltpu.VMEM)
    scalar = pl.BlockSpec(memory_space=pltpu.SMEM)
    return pl.pallas_call(
        kernel,
        out_shape=out_shape,
        in_specs=[scalar] * scalars
        + [vmem] * (len(args) - scalars - unread)
        + [pl.BlockSpec(memory_space=pl.ANY)] * unread,
        out_specs=jax.tree.map(lambda _: vmem, out_shape),
        scratch_shapes=list(scratch),
        cost_estimate=pl.CostEstimate(flops=flops, bytes_accessed=0, transcendentals=0),
        compiler_params=pltpu.CompilerParams(vmem_limit_bytes=20 << 20),
    )(*args)


def swap(x, axis):
    return lax.ppermute(x, axis, [(0, 1), (1, 0)])


def per_device(frames, basis):
    rows, width = frames.shape
    vecs = basis.shape[1]
    n_time, n_feat = lax.axis_size(TIME), lax.axis_size(FEAT)
    n_z = 2 * lax.axis_size("zh")
    block, part = lax.axis_index(TIME), lax.axis_index(FEAT)
    frames_counted = 2.0 * rows * (n_time - 1)
    count = jnp.where((block == 0) | (block == n_time - 1), 1.0, 2.0)
    f32, bf16 = jnp.float32, jnp.bfloat16

    core, xlo = lax.axis_index("core"), lax.axis_index("xlo")

    piece = rows // n_feat
    owned = width // n_time
    projected = dot(frames, basis, precision=None)
    local = jnp.mean(projected, axis=0)
    high = lax.reduce_precision(local, 8, 7)
    middle = lax.reduce_precision(local - high, 8, 7)
    low = local - high - middle
    terms = jnp.stack([high, middle, low]).astype(bf16)
    terms = jnp.concatenate([terms, jnp.zeros((13, vecs), bf16)], axis=0)
    packed = jnp.concatenate(
        [
            (projected - local).astype(bf16).reshape(n_feat, piece, vecs),
            jnp.broadcast_to(terms, (n_feat, 16, vecs)),
        ],
        axis=1,
    )
    shift = call(shift_kernel, jax.ShapeDtypeStruct((n_time, 128), f32), frames)
    packed = lax.all_to_all(packed, FEAT, 0, 0, tiled=True)

    centred, offset = call(
        collect_kernel,
        [
            jax.ShapeDtypeStruct((n_feat, piece, vecs), bf16),
            jax.ShapeDtypeStruct((8, vecs), f32),
        ],
        packed,
    )
    centred = lax.all_to_all(centred, FEAT, 0, 0, tiled=True).reshape(rows, vecs)
    pairs = [(i, i + 1) for i in range(1, n_time - 1, 2)]
    across_chips = lax.ppermute(centred, TIME, pairs + [(b, a) for a, b in pairs])
    on_chip = lax.all_gather(centred, "core")

    gram_rows = 2 * vecs // n_feat
    each = gram_rows // n_time
    cols = vecs // n_feat
    wide = vecs - (-(2 * cols + owned) // 128) * 128
    sent, beside = call(
        gram_kernel,
        [
            jax.ShapeDtypeStruct((n_time, each, wide), f32),
            jax.ShapeDtypeStruct((8, vecs), f32),
        ],
        jnp.stack([part, jnp.int32(n_feat), count.astype(jnp.int32), core]),
        centred,
        on_chip,
        across_chips,
        offset,
        shift,
        scalars=1,
        scratch=[pltpu.VMEM((vecs, vecs), f32)],
    )
    got = lax.all_to_all(sent, TIME, 0, 0, tiled=True)
    gram, sums, shifts = call(
        total_kernel,
        [
            jax.ShapeDtypeStruct((n_time // 2, each, vecs), f32),
            jax.ShapeDtypeStruct((n_time, 2 * cols), f32),
            jax.ShapeDtypeStruct((n_time, owned), f32),
        ],
        got,
    )
    half = (2 * n_z, owned, vecs)
    kept, given = call(
        contract_kernel,
        [jax.ShapeDtypeStruct(half, f32), jax.ShapeDtypeStruct(half, bf16)],
        core[None],
        frames,
        on_chip,
        across_chips,
        beside,
        scalars=1,
        flops=4 * rows * width * vecs,
    )
    place = (2, n_z // 2, 2, owned, vecs)
    mine, given = call(
        lambda *refs: halve_kernel(0, *refs),
        [jax.ShapeDtypeStruct(place[1:], f32), jax.ShapeDtypeStruct(place[1:], bf16)],
        xlo[None],
        kept.reshape(place),
        swap(given, "core").reshape(place),
        scalars=1,
    )

    gram = lax.all_to_all(gram, ("zh", "zl", "core"), 0, 0, tiled=True)
    slices = call(
        slices_kernel,
        jax.ShapeDtypeStruct((2 * n_feat, gram_rows // 2 + 8, vecs), f32),
        xlo[None],
        gram,
        sums,
        mine,
        scalars=1,
        unread=1,
    )
    slices = lax.all_to_all(slices, ("xlo",) + FEAT, 0, 0, tiled=True)

    mine, given = call(
        lambda *refs: halve_kernel(1, *refs),
        [
            jax.ShapeDtypeStruct((n_z // 2, owned, vecs), f32),
            jax.ShapeDtypeStruct((n_z // 2, owned, vecs), bf16),
        ],
        lax.axis_index("zl")[None],
        mine,
        swap(given, "xlo"),
        scalars=1,
    )
    lagged = (mine + swap(given, "zl").astype(f32)).astype(bf16)
    lagged = lax.all_to_all(lagged, "zh", 0, 0, tiled=True)

    square = jax.ShapeDtypeStruct((vecs, vecs), f32)
    inv, reduced, edge, share = call(
        lambda *refs: whiten_kernel(n_time, frames_counted, *refs),
        [
            square,
            square,
            jax.ShapeDtypeStruct((n_time, vecs), f32),
            jax.ShapeDtypeStruct((n_time, 128), f32),
        ],
        slices,
        flops=11 * 10**9,
    )
    new_basis = call(
        lambda *refs: finish_kernel(frames_counted, *refs),
        jax.ShapeDtypeStruct((owned, vecs), f32),
        lagged,
        shifts,
        edge,
        share,
        inv,
        flops=10**9,
    )
    return (new_basis, reduced)


def solution(mesh):
    n_time, n_feat = mesh.devices.shape
    mesh = Mesh(mesh.devices.reshape(2, n_time // 8, 2, 2, 2, n_feat // 2), TIME + FEAT)
    return jax.shard_map(
        per_device,
        mesh=mesh,
        in_specs=(P(TIME, FEAT), P(FEAT, None)),
        out_specs=(P(FEAT + TIME, None), P()),
        check_vma=False,
    )
```

```python
import jax
import jax.numpy as jnp
from jax import lax
from jax.experimental import pallas as pl
from jax.experimental.pallas import tpu as pltpu
from jax.sharding import Mesh, PartitionSpec as P

TIME = ("xlo", "zh", "zl", "core")
FEAT = ("xhi", "y")
EXACT = lax.Precision.HIGHEST


def dot(a, b, dims=((1,), (0,)), precision=EXACT):
    return lax.dot_general(
        a, b, (dims, ((), ())), precision=precision, preferred_element_type=jnp.float32
    )


def inverse_factor(block):
    nb = block.shape[0]
    wide, count = 2 * nb, nb // 8
    lanes = lax.broadcasted_iota(jnp.int32, (8, nb), 1)
    subs = lax.broadcasted_iota(jnp.int32, (8, nb), 0)
    below = lax.broadcasted_iota(jnp.int32, (8, wide), 0)
    tiles = [
        jnp.concatenate(
            [block[8 * g : 8 * g + 8], (lanes == subs + 8 * g).astype(jnp.float32)], axis=1
        )
        for g in range(count)
    ]
    out = []
    for g in range(count):
        spread = [
            [jnp.broadcast_to(tiles[i][:, 8 * g + k : 8 * g + k + 1], (8, wide)) for i in range(g, count)]
            for k in range(8)
        ]
        rows = tiles[g]
        for r in range(0, 8, 2):
            c0, c1 = spread[r], spread[r + 1]
            p, q, s = c0[0][r : r + 1], c1[0][r : r + 1], c1[0][r + 1 : r + 2]
            det = p * s - q * q
            inv = 1.0 / det
            pi, qi, si = p * inv, q * inv, s * inv
            for k in range(r + 2, 8):
                x, y = spread[k][0][r : r + 1], spread[k][0][r + 1 : r + 2]
                gx, gy = si * x - qi * y, pi * y - qi * x
                for i in range(count - g):
                    spread[k][i] = spread[k][i] - (c0[i] * gx + c1[i] * gy)
            a, b = rows[r : r + 1], rows[r + 1 : r + 2]
            v = p * b - q * a
            ga, gb = si * a - qi * b, v * inv
            out.append(a * lax.rsqrt(p))
            out.append(v * lax.rsqrt(p * det))
            if r < 6:
                keep = below > r + 1
                rows = rows - (jnp.where(keep, c0[0], 0.0) * ga + jnp.where(keep, c1[0], 0.0) * gb)
            for i in range(g + 1, count):
                tiles[i] = tiles[i] - (c0[i - g] * ga + c1[i - g] * gb)
    return jnp.concatenate(out, axis=0)[:, nb:]


def inverse_cholesky(a, nb):
    n = a.shape[0]
    eye = lax.broadcasted_iota(jnp.int32, (n, n), 0) == lax.broadcasted_iota(jnp.int32, (n, n), 1)
    diagonal = jnp.where(eye, a, 0.0)
    down = lax.rsqrt(jnp.sum(diagonal, axis=1, keepdims=True))
    along = lax.rsqrt(jnp.sum(diagonal, axis=0, keepdims=True))
    left, right = a * down * along, eye.astype(jnp.float32)
    rows = []
    for b in range(n // nb):
        start = nb * b // 128 * 128
        stop = min(n, -(-nb * (b + 1) // 128) * 128)
        left = left[:, start - n :]
        at = nb * b - start
        t = inverse_factor(left[:nb, at : at + nb])
        both = jnp.concatenate([left, right[:, :stop]], axis=1)
        p = dot(t, both[:nb])
        here = p[:, n - start :]
        rows.append(here if stop == n else jnp.concatenate([here, right[:nb, stop:]], axis=1))
        if nb * (b + 1) < n:
            both = both[nb:] - dot(p[:, at + nb : n - start], p, ((0,), (0,)))
            left = both[:, : n - start]
            right_done, right_rest = both[:, n - start :], right[nb:]
            right = right_done
            if stop < n:
                right = jnp.concatenate([right_done, right_rest[:, stop:]], axis=1)
    return jnp.concatenate(rows, axis=0) * along


def whiten_kernel(blocks, frames_counted, g_ref, inv_ref, reduced_ref, edge_ref, mean_ref):
    peers, height, vecs = g_ref.shape
    n_feat, rows = peers // 2, height - 8
    part, half = vecs // n_feat, n_feat // 2

    def joined(start):
        return jnp.concatenate(
            [g_ref[x * n_feat + start + k, :rows] for k in range(half) for x in range(2)], axis=0
        )

    def sums(start):
        columns = []
        for k in range(n_feat):
            side = [g_ref[x * n_feat + k, rows:] for x in range(2)]
            columns.append(
                jnp.concatenate(
                    [
                        side[x][:, 2 * part * g + start : 2 * part * g + start + part]
                        for x in range(2)
                        for g in range(blocks // 16)
                    ],
                    axis=0,
                )
            )
        return jnp.concatenate(columns, axis=1)

    gram0, gram1 = joined(0), joined(half)
    u, z = sums(0), sums(part)
    size = frames_counted / (2.0 * blocks - 2.0)
    ids = lax.broadcasted_iota(jnp.int32, (blocks, 1), 0)
    count = jnp.where((ids == 0) | (ids == blocks - 1), 1.0, 2.0)
    share = count / (2.0 * blocks - 2.0)
    d = u - jnp.sum(share * u, axis=0, keepdims=True)
    y = z + size * d
    nothing = jnp.zeros((1, vecs), jnp.float32)

    def neighbours(x):
        return jnp.concatenate([x[1:], nothing], axis=0) + jnp.concatenate([nothing, x[:-1]], axis=0)

    edge = neighbours(y)
    edge_ref[...] = edge
    mean_ref[...] = jnp.broadcast_to(share, mean_ref.shape)
    across = ((0,), (0,))
    gram0 = (gram0 + dot(d, count * y, across) + dot(z, count * d, across)) / frames_counted
    gram1 = (gram1 + dot(z, neighbours(d), across) + dot(d, edge, across)) / frames_counted
    inv = inverse_cholesky((gram0 + gram0.T) * 0.5, 64)
    inv_ref[...] = inv
    reduced_ref[...] = dot(dot(inv, gram1), inv, ((1,), (1,)))


def finish_kernel(frames_counted, sum_ref, shift_ref, edge_ref, share_ref, inv_ref, out_ref):
    shift = shift_ref[...]
    shift = shift - jnp.sum(share_ref[:, :1] * shift, axis=0, keepdims=True)
    lagged = jnp.sum(sum_ref[...].astype(jnp.float32), axis=0) + dot(shift, edge_ref[...], ((0,), (0,)))
    out_ref[...] = dot(lagged / frames_counted, inv_ref[...], ((1,), (1,)))


def shift_kernel(frames_ref, out_ref):
    n_time, lanes = out_ref.shape
    rows, width = frames_ref.shape
    owned = width // n_time
    step = width // 4
    hit = lax.broadcasted_iota(jnp.int32, (owned, lanes), 0) == lax.broadcasted_iota(
        jnp.int32, (owned, lanes), 1
    )
    ones = jnp.ones((rows, lanes), jnp.bfloat16)
    for i in range(4):
        sums = dot(frames_ref[:, i * step : (i + 1) * step], ones, ((0,), (0,)), None)
        sums = jnp.where(hit[None], sums.reshape(step // owned, owned, lanes), 0.0)
        rows_here = n_time // 4
        out_ref[i * rows_here : (i + 1) * rows_here] = jnp.sum(sums, axis=1) / rows


def collect_kernel(got_ref, centred_ref, offset_ref):
    piece = centred_ref.shape[1]
    total = jnp.sum(got_ref[...].astype(jnp.float32), axis=0)
    offset = jnp.sum(total[piece:], axis=0, keepdims=True)
    offset_ref[...] = jnp.broadcast_to(offset, offset_ref.shape)
    centred_ref[...] = jnp.broadcast_to(total[:piece].astype(jnp.bfloat16)[None], centred_ref.shape)


def gram_kernel(
    place_ref, centred_ref, first_ref, second_ref, offset_ref, shift_ref, sent_ref, beside_ref, gram_ref
):
    n_time, each, wide = sent_ref.shape
    vecs = gram_ref.shape[0]
    part, n_feat, count = place_ref[0], place_ref[1], place_ref[2]
    half = n_feat // 2
    across = ((0,), (0,))
    first, second = first_ref[1 - place_ref[3]], second_ref[...]
    beside = jnp.sum(first.astype(jnp.float32), axis=0, keepdims=True) + jnp.sum(
        second.astype(jnp.float32), axis=0, keepdims=True
    )
    beside_ref[...] = jnp.broadcast_to(beside, beside_ref.shape)

    @pl.when(part < half)
    def _():
        gram_ref[...] = count.astype(jnp.float32) * dot(
            centred_ref[...], centred_ref[...], across, None
        )

    @pl.when(part >= half)
    def _():
        gram_ref[...] = dot(centred_ref[...], first, across, None) + dot(
            centred_ref[...], second, across, None
        )

    rows = n_time * each
    mine = gram_ref[pl.ds(pl.multiple_of(lax.rem(part, half) * rows, rows), rows), :]
    part_cols = rows // 2
    total = jnp.sum(centred_ref[...].astype(jnp.float32), axis=0, keepdims=True)
    both = jnp.concatenate(
        [offset_ref[:4], jnp.broadcast_to(total, (4, vecs))], axis=0
    )
    both = pltpu.roll(both, lax.rem(n_feat - part, n_feat) * part_cols, 1)[:, :part_cols]
    extra = jnp.concatenate(
        [
            jnp.broadcast_to(both[:1], (n_time, part_cols)),
            jnp.broadcast_to(both[4:5], (n_time, part_cols)),
            shift_ref[:, : wide - vecs - 2 * part_cols],
        ],
        axis=1,
    )
    for i in range(n_time):
        sent_ref[i, :, :vecs] = mine[i * each : (i + 1) * each]
        sent_ref[i, :, vecs:] = jnp.broadcast_to(extra[i : i + 1], (each, wide - vecs))


def total_kernel(got_ref, row_ref, sums_ref, shift_ref):
    copies, _, vecs = row_ref.shape
    n_time = sums_ref.shape[0]
    total = got_ref[0, :, :vecs]
    for i in range(1, n_time):
        total = total + got_ref[i, :, :vecs]
    for i in range(copies):
        row_ref[i] = total
    low = vecs + sums_ref.shape[1]
    for i in range(n_time):
        sums_ref[i : i + 1] = got_ref[i, :1, vecs:low]
        shift_ref[i : i + 1] = got_ref[i, :1, low : low + shift_ref.shape[1]]


def slices_kernel(xlo_ref, rows_ref, sums_ref, _, out_ref):
    copies, height, vecs = out_ref.shape
    blocks, each, _ = rows_ref.shape
    for i in range(blocks):
        out_ref[0, i * each : (i + 1) * each] = rows_ref[i]
    first = pl.multiple_of(xlo_ref[0] * blocks, 8)
    side = [sums_ref[pl.ds(first + 8 * g, 8), :] for g in range(blocks // 8)]
    rest = vecs - len(side) * sums_ref.shape[1]
    side = side + [jnp.zeros((8, rest), jnp.float32)] if rest else side
    out_ref[0, height - 8 :] = jnp.concatenate(side, axis=1)
    for k in range(1, copies):
        out_ref[k] = out_ref[0]


def contract_kernel(core_ref, frames_ref, first_ref, second_ref, beside_ref, kept_ref, given_ref):
    owned, vecs = kept_ref.shape[1:]
    rows, width = frames_ref.shape
    groups = 4
    core = core_ref[0]
    beside = beside_ref[:1] / rows
    right = jnp.concatenate(
        [first_ref[1 - core], second_ref[...], jnp.ones((rows, 128), jnp.bfloat16)], axis=1
    )
    step = 2 * groups * owned
    for i in range(width // step):
        sums = dot(frames_ref[:, i * step : (i + 1) * step], right, ((0,), (0,)), None)
        total = jnp.concatenate([sums[:, 2 * vecs :]] * (vecs // 128), axis=1)
        sums = sums[:, :vecs] + sums[:, vecs : 2 * vecs] - total * beside
        sums = sums.reshape(groups, 2, owned, vecs)
        low, high = sums[:, 0], sums[:, 1]
        part = slice(i * groups, (i + 1) * groups)
        kept_ref[part] = jnp.where(core == 0, low, high).astype(kept_ref.dtype)
        given_ref[part] = jnp.where(core == 0, high, low).astype(given_ref.dtype)


def halve_kernel(axis, place_ref, kept_ref, got_ref, mine_ref, given_ref):
    def at(which):
        return (slice(None),) * axis + (which,)

    own, other = at(place_ref[0]), at(1 - place_ref[0])
    mine_ref[...] = kept_ref[own].astype(jnp.float32) + got_ref[own].astype(jnp.float32)
    given_ref[...] = (kept_ref[other].astype(jnp.float32) + got_ref[other].astype(jnp.float32)).astype(given_ref.dtype)


def call(kernel, out_shape, *args, scalars=0, unread=0, scratch=(), flops=0):
    vmem = pl.BlockSpec(memory_space=pltpu.VMEM)
    scalar = pl.BlockSpec(memory_space=pltpu.SMEM)
    return pl.pallas_call(
        kernel,
        out_shape=out_shape,
        in_specs=[scalar] * scalars
        + [vmem] * (len(args) - scalars - unread)
        + [pl.BlockSpec(memory_space=pl.ANY)] * unread,
        out_specs=jax.tree.map(lambda _: vmem, out_shape),
        scratch_shapes=list(scratch),
        cost_estimate=pl.CostEstimate(flops=flops, bytes_accessed=0, transcendentals=0),
        compiler_params=pltpu.CompilerParams(vmem_limit_bytes=20 << 20),
    )(*args)


def swap(x, axis):
    return lax.ppermute(x, axis, [(0, 1), (1, 0)])


def per_device(frames, basis):
    rows, width = frames.shape
    vecs = basis.shape[1]
    n_time, n_feat = lax.axis_size(TIME), lax.axis_size(FEAT)
    n_z = 2 * lax.axis_size("zh")
    block, part = lax.axis_index(TIME), lax.axis_index(FEAT)
    frames_counted = 2.0 * rows * (n_time - 1)
    count = jnp.where((block == 0) | (block == n_time - 1), 1.0, 2.0)
    f32, bf16 = jnp.float32, jnp.bfloat16

    core, xlo = lax.axis_index("core"), lax.axis_index("xlo")

    piece = rows // n_feat
    owned = width // n_time
    projected = dot(frames, basis, precision=None)
    local = jnp.mean(projected, axis=0)
    high = lax.reduce_precision(local, 8, 7)
    middle = lax.reduce_precision(local - high, 8, 7)
    low = local - high - middle
    terms = jnp.stack([high, middle, low]).astype(bf16)
    terms = jnp.concatenate([terms, jnp.zeros((13, vecs), bf16)], axis=0)
    packed = jnp.concatenate(
        [
            (projected - local).astype(bf16).reshape(n_feat, piece, vecs),
            jnp.broadcast_to(terms, (n_feat, 16, vecs)),
        ],
        axis=1,
    )
    shift = call(shift_kernel, jax.ShapeDtypeStruct((n_time, 128), f32), frames)
    packed = lax.all_to_all(packed, FEAT, 0, 0, tiled=True)

    centred, offset = call(
        collect_kernel,
        [
            jax.ShapeDtypeStruct((n_feat, piece, vecs), bf16),
            jax.ShapeDtypeStruct((8, vecs), f32),
        ],
        packed,
    )
    centred = lax.all_to_all(centred, FEAT, 0, 0, tiled=True).reshape(rows, vecs)
    pairs = [(i, i + 1) for i in range(1, n_time - 1, 2)]
    across_chips = lax.ppermute(centred, TIME, pairs + [(b, a) for a, b in pairs])
    on_chip = lax.all_gather(centred, "core")

    gram_rows = 2 * vecs // n_feat
    each = gram_rows // n_time
    cols = vecs // n_feat
    wide = vecs - (-(2 * cols + owned) // 128) * 128
    sent, beside = call(
        gram_kernel,
        [
            jax.ShapeDtypeStruct((n_time, each, wide), f32),
            jax.ShapeDtypeStruct((8, vecs), f32),
        ],
        jnp.stack([part, jnp.int32(n_feat), count.astype(jnp.int32), core]),
        centred,
        on_chip,
        across_chips,
        offset,
        shift,
        scalars=1,
        scratch=[pltpu.VMEM((vecs, vecs), f32)],
    )
    got = lax.all_to_all(sent, TIME, 0, 0, tiled=True)
    gram, sums, shifts = call(
        total_kernel,
        [
            jax.ShapeDtypeStruct((n_time // 2, each, vecs), f32),
            jax.ShapeDtypeStruct((n_time, 2 * cols), f32),
            jax.ShapeDtypeStruct((n_time, owned), f32),
        ],
        got,
    )
    half = (2 * n_z, owned, vecs)
    kept, given = call(
        contract_kernel,
        [jax.ShapeDtypeStruct(half, bf16), jax.ShapeDtypeStruct(half, bf16)],
        core[None],
        frames,
        on_chip,
        across_chips,
        beside,
        scalars=1,
        flops=4 * rows * width * vecs,
    )
    place = (2, n_z // 2, 2, owned, vecs)
    mine, given = call(
        lambda *refs: halve_kernel(0, *refs),
        [jax.ShapeDtypeStruct(place[1:], f32), jax.ShapeDtypeStruct(place[1:], bf16)],
        xlo[None],
        kept.reshape(place),
        swap(given, "core").reshape(place),
        scalars=1,
    )

    gram = lax.all_to_all(gram, ("zh", "zl", "core"), 0, 0, tiled=True)
    slices = call(
        slices_kernel,
        jax.ShapeDtypeStruct((2 * n_feat, gram_rows // 2 + 8, vecs), f32),
        xlo[None],
        gram,
        sums,
        mine,
        scalars=1,
        unread=1,
    )
    slices = lax.all_to_all(slices, ("xlo",) + FEAT, 0, 0, tiled=True)

    mine, given = call(
        lambda *refs: halve_kernel(1, *refs),
        [
            jax.ShapeDtypeStruct((n_z // 2, owned, vecs), f32),
            jax.ShapeDtypeStruct((n_z // 2, owned, vecs), bf16),
        ],
        lax.axis_index("zl")[None],
        mine,
        swap(given, "xlo"),
        scalars=1,
    )
    lagged = (mine + swap(given, "zl").astype(f32)).astype(bf16)
    lagged = lax.all_to_all(lagged, "zh", 0, 0, tiled=True)

    square = jax.ShapeDtypeStruct((vecs, vecs), f32)
    inv, reduced, edge, share = call(
        lambda *refs: whiten_kernel(n_time, frames_counted, *refs),
        [
            square,
            square,
            jax.ShapeDtypeStruct((n_time, vecs), f32),
            jax.ShapeDtypeStruct((n_time, 128), f32),
        ],
        slices,
        flops=11 * 10**9,
    )
    new_basis = call(
        lambda *refs: finish_kernel(frames_counted, *refs),
        jax.ShapeDtypeStruct((owned, vecs), f32),
        lagged,
        shifts,
        edge,
        share,
        inv,
        flops=10**9,
    )
    return (new_basis, reduced)


def solution(mesh):
    n_time, n_feat = mesh.devices.shape
    mesh = Mesh(mesh.devices.reshape(2, n_time // 8, 2, 2, 2, n_feat // 2), TIME + FEAT)
    return jax.shard_map(
        per_device,
        mesh=mesh,
        in_specs=(P(TIME, FEAT), P(FEAT, None)),
        out_specs=(P(FEAT + TIME, None), P()),
        check_vma=False,
    )
```
